32 devices in a mesh: seq: 8 (over z, y), ch: 4 (over x, core).
Axes of the slice: x: 2, y: 2, z: 4, core: 2. Of those that a mesh axis runs over, the one named last changes fastest.
Arguments:
- query_proj: bfloat16 [4096, 512], P('seq', 'ch'), may hold values from -6 to 6
- key_proj: bfloat16 [4096, 512], P('seq', 'ch'), may hold values from -6 to 6
- value_proj: bfloat16 [4096, 512], P('seq', 'ch'), may hold values from -6 to 6
- filter_taps: float32 [4096, 128], P('seq'), may hold values from -1.1 to 1.1, as said below
- skip_gain: float32 [512], P('ch'), may hold values from 0.3 to 3
- grad_mixer: bfloat16 [4096, 512], P('seq', 'ch'), may hold values from -6 to 6
Outputs:
- mixer_out: bfloat16 [4096, 512], P('seq', 'ch')
- grad_query: bfloat16 [4096, 512], P('seq', 'ch')
- grad_key: bfloat16 [4096, 512], P('seq', 'ch')
- grad_value: bfloat16 [4096, 512], P('seq', 'ch')
- grad_filter: float32 [4096, 128], P('seq', 'ch')
The draws below stay inside these ranges and needn't reach their ends.
Inputs may be any that keep to these rules, and one draw needn't show every extreme that they name: `filter_taps`: real-valued filter taps.
All inputs are finite; a program needn't handle non-finite values.
Results may differ from the reference program's by a relative error of at most 0.001.
Values sent between devices are 32-bit elements; how exact they have to be, the bound alone decides.
A program may use at most 64 MiB of HBM per device.

```python
import math
import jax
import jax.numpy as jnp

CH = 512
KERNEL_GROUPS = 128
SEQUENCE_STEPS = 4096


def draw_filter_taps(key, part):
    seed_jitter_samples, seed_extent, seed_spike_samples, seed_masking = jax.random.split(key, 4)
    delay_shifts = jnp.arange(SEQUENCE_STEPS, dtype=jnp.float32)[:, None]
    low_log = math.log(30.0)
    high_log = math.log(4.0 * SEQUENCE_STEPS)
    noise = jax.random.truncated_normal(seed_jitter_samples, -4.0, 4.0, (SEQUENCE_STEPS, KERNEL_GROUPS), jnp.float32)
    reach = jnp.exp(jax.random.uniform(seed_extent, (1, KERNEL_GROUPS), jnp.float32, low_log, high_log))
    decay = jnp.exp(-delay_shifts / reach)
    spike_occurrences = jax.random.randint(seed_spike_samples, (3, 1, KERNEL_GROUPS), 1, SEQUENCE_STEPS).astype(jnp.float32)
    successful_tests = jnp.sum((delay_shifts[None, :, :] >= spike_occurrences).astype(jnp.float32), axis=0)
    keep = jax.random.uniform(seed_masking, (1, KERNEL_GROUPS), jnp.float32, 0.5, 0.8)
    norm_factor = jnp.sqrt(2.0 / (reach * (1.0 - jnp.exp(-2.0 * SEQUENCE_STEPS / reach))))
    return (noise * decay * keep ** successful_tests * norm_factor).astype(jnp.float32)


def level_of(stream_key, shape, cuts, least, top_value):
    loudness, own = 1.0, jax.random.fold_in(stream_key, 6)
    for position, blocks in cuts:
        steps = jnp.exp(jax.random.uniform(jax.random.fold_in(own, position), (blocks,), jnp.float32, least / len(cuts), top_value / len(cuts)))
        loudness = loudness * jnp.repeat(steps, shape[position] // blocks).reshape([-1 if axis == position else 1 for axis in range(len(shape))])
    return loudness


def scatter_about(own_key, extent, scale, most, shards=(), kind=jnp.bfloat16):
    entries = scale * jax.random.normal(own_key, extent, jnp.float32)
    if shards:
        entries = entries * level_of(own_key, extent, shards, -0.22, 0.18)
    return jnp.clip(entries, -most, most).astype(kind)


def setup_inputs(seed: int = 0) -> dict:
    key_list = jax.random.split(jax.random.key(seed), 7)
    query_proj = scatter_about(key_list[0], (SEQUENCE_STEPS, CH), 1.0, 6.0, ((0, 8), (1, 4)))
    key_proj = scatter_about(key_list[1], (SEQUENCE_STEPS, CH), 1.0, 6.0, ((0, 8), (1, 4)))
    value_proj = scatter_about(key_list[2], (SEQUENCE_STEPS, CH), 1.0, 6.0, ((0, 8), (1, 4)))
    filter_taps = draw_filter_taps(jax.random.fold_in(key_list[6], 71), 0)
    skip_gain = jnp.clip(jnp.exp(math.log(3.0) - 2.3025851 * jax.random.uniform(key_list[4], (CH,), jnp.float32) ** level_of(key_list[4], (CH,), ((0, 4),), -0.2, 0.2)), 0.3, 3.0)
    grad_mixer = scatter_about(key_list[5], (SEQUENCE_STEPS, CH), 1.0, 6.0, ((0, 8), (1, 4)))
    return {"query_proj": query_proj, "key_proj": key_proj, "value_proj": value_proj, "filter_taps": filter_taps, "skip_gain": skip_gain, "grad_mixer": grad_mixer}


def causal_conv(taps, signal):
    length = 2 * SEQUENCE_STEPS
    taps_hat = jnp.fft.rfft(taps, n=length, axis=0)
    signal_hat = jnp.fft.rfft(signal, n=length, axis=0)
    return jnp.fft.irfft(taps_hat * signal_hat, n=length, axis=0)[:SEQUENCE_STEPS]


def correlate(first, second):
    length = 2 * SEQUENCE_STEPS
    first_hat = jnp.fft.rfft(first, n=length, axis=0)
    second_hat = jnp.fft.rfft(second, n=length, axis=0)
    return jnp.fft.irfft(jnp.conj(first_hat) * second_hat, n=length, axis=0)[:SEQUENCE_STEPS]


def reference(query_proj, key_proj, value_proj, filter_taps, skip_gain, grad_mixer):
    repeats = CH // KERNEL_GROUPS
    taps_full = jnp.tile(filter_taps, (1, repeats))
    query = query_proj.astype(jnp.float32)
    key_data = key_proj.astype(jnp.float32)
    value_data = value_proj.astype(jnp.float32)
    upstream = grad_mixer.astype(jnp.float32)
    mixed = key_data * value_data
    conv = causal_conv(taps_full, mixed)
    pre = conv + skip_gain[None, :] * mixed
    mixer_out = (query * pre).astype(jnp.bfloat16)
    grad_in = upstream * query
    grad_query = (upstream * pre).astype(jnp.bfloat16)
    back = correlate(taps_full, grad_in) + skip_gain[None, :] * grad_in
    grad_key = (back * value_data).astype(jnp.bfloat16)
    grad_value = (back * key_data).astype(jnp.bfloat16)
    per_channel = correlate(mixed, grad_in)
    grad_filter = per_channel.reshape(SEQUENCE_STEPS, repeats, KERNEL_GROUPS).sum(axis=1) * (SEQUENCE_STEPS ** -0.5)
    return mixer_out, grad_query, grad_key, grad_value, grad_filter
```

```python
import functools
import math

import jax
import jax.numpy as jnp
import ml_dtypes
import numpy as np
from jax import lax
from jax.experimental import pallas as pl
from jax.experimental.pallas import tpu as pltpu
from jax.sharding import PartitionSpec as P

MESH = pl.DeviceIdType.MESH
LANES = 128


def halves(table):
    head = table.astype(np.float32).astype(ml_dtypes.bfloat16)
    tail = (table - head.astype(np.float64)).astype(np.float32).astype(ml_dtypes.bfloat16)
    return np.stack([head, tail])


@functools.lru_cache(maxsize=4)
def tables(seq_count, ch_count, nb, filters):
    ndev = seq_count * ch_count
    nf = filters // ndev
    dup = max(1, 8 // (nb * nf))
    n1 = seq_count * nb
    total = n1 * LANES
    a = np.arange(n1)
    ang = 2 * np.pi / n1 * ((a[:, None] + 0.25) * a[None, :])
    stack = np.concatenate([np.cos(ang), -np.sin(ang)], 0)
    first = np.kron(stack, np.eye(2 * nf))
    pick = np.kron(np.array([[1.0], [1.0]]), np.kron(np.eye(dup)[:1], np.eye(nf)))
    first_taps = np.kron(stack, pick)
    last = first.T / total
    keep = np.kron(np.ones((dup, 1)), np.concatenate([np.eye(nf), np.zeros((nf, nf))], 1))
    last_filt = np.kron(stack.T, keep) / total / math.sqrt(total)
    b = np.arange(LANES)
    turn = 2 * np.pi / total * ((a[:, None] + 0.25) * b[None, :])
    twist = np.repeat(np.stack([np.cos(turn), -np.sin(turn)]), 2 * nf, axis=1)
    ang2 = 2 * np.pi / LANES * (b[:, None] * b[None, :] % LANES)
    fr, fi = np.cos(ang2), -np.sin(ang2)
    second = np.block([[fr, fi], [-fi, fr]])
    d, kind, f = np.meshgrid(np.arange(ndev), np.arange(2), np.arange(nf), indexing="ij")
    perm = np.zeros((ndev, 2 * nf, 2 * filters))
    perm[d, kind * nf + f, kind * filters + d * nf + f] = 1.0
    if 2 * nf % 8:
        wide = np.zeros((nb, ndev, nb, 2 * nf, 2 * filters))
        for j in range(nb):
            wide[j, :, j] = perm
        perm = wide.reshape(nb, ndev * nb * 2 * nf, 2 * filters)
    else:
        perm = perm.reshape(1, ndev * 2 * nf, 2 * filters)
    perm_taps = np.zeros((nb, ndev, nb, dup, nf, filters))
    own = filters // ch_count // nf
    sel = np.zeros((nb, own, nb, dup, nf, LANES))
    for j in range(nb):
        for g in range(nf):
            for dev in range(ndev):
                perm_taps[j, dev, j, :, g, dev * nf + g] = 1.0
            for dev in range(own):
                sel[j, dev, j, 0, g, dev * nf + g] = 1.0
    bf = ml_dtypes.bfloat16
    return (
        perm.astype(bf),
        perm_taps.reshape(nb, ndev * nb * dup * nf, filters).astype(bf),
        sel.reshape(nb, own * nb * dup * nf, LANES).astype(bf),
        halves(first),
        halves(first_taps),
        halves(last),
        halves(last_filt),
        halves(second),
        halves(second.T),
        twist.astype(np.float32),
    )


def split(x):
    head = x.astype(jnp.bfloat16)
    return head, (x - head.astype(jnp.float32)).astype(jnp.bfloat16)


def mm(x, y):
    return jnp.dot(x, y, preferred_element_type=jnp.float32)


def mm_nt(x, y):
    return lax.dot_general(x, y, (((1,), (1,)), ((), ())), preferred_element_type=jnp.float32)


def left_table(table, x):
    hi, lo = split(x)
    return mm(table[0], hi) + mm(table[0], lo) + mm(table[1], hi)


def right_table(x, table):
    hi, lo = split(x)
    return mm(hi, table[0]) + mm(lo, table[0]) + mm(hi, table[1])


def kernel(
    seq_count, ch_count, nf,
    q_ref, k_ref, v_ref, h_ref, gain_ref, u_ref,
    perm, perm_taps, sel, first, first_taps, last, last_filt, second, second_t, twist,
    mix_ref, gq_ref, gk_ref, gv_ref, gf_ref,
    tx, rx, txh, rxh, txo, rxo, txf, rxf,
    send_a, recv_a, send_h, recv_h, send_o, recv_o, send_f, recv_f,
):
    ndev = seq_count * ch_count
    local_rows, filters = h_ref.shape
    nb = local_rows // LANES
    q = 2 * nf
    own = rxf.shape[0]
    rows = seq_count * nb * q
    s, c = lax.axis_index("seq"), lax.axis_index("ch")
    me = s * ch_count + c
    f32 = jnp.float32

    barrier = pltpu.get_barrier_semaphore()

    def greet(i, _):
        p = lax.rem(me + i, ndev)
        pl.semaphore_signal(
            barrier, inc=1, device_id=(p // ch_count, lax.rem(p, ch_count)), device_id_type=MESH
        )
        return 0

    lax.fori_loop(1, ndev, greet, 0)

    acc = None
    for j in range(nb):
        hi, lo = split(h_ref[pl.ds(j * LANES, LANES), :])
        part = mm_nt(perm_taps[j], hi) + mm_nt(perm_taps[j], lo)
        acc = part if acc is None else acc + part
    txh[...] = acc.reshape(txh.shape)
    acc = None
    for j in range(nb):
        r = pl.ds(j * LANES, LANES)
        m = k_ref[r, :].astype(f32) * v_ref[r, :].astype(f32)
        g = u_ref[r, :].astype(f32) * q_ref[r, :].astype(f32)
        hi, lo = split(jnp.concatenate([m, g], axis=1))
        if perm.shape[0] == 1:
            part = mm_nt(perm[0], hi) + mm_nt(perm[0], lo)
            tx[:, j * q : (j + 1) * q, :] = part.reshape(ndev, q, LANES)
        else:
            part = mm_nt(perm[j], hi) + mm_nt(perm[j], lo)
            acc = part if acc is None else acc + part
    if acc is not None:
        tx[...] = acc.reshape(tx.shape)

    def copy_a(p, src):
        return pltpu.make_async_remote_copy(
            src_ref=tx.at[p],
            dst_ref=rx.at[lax.rem(src, ch_count), src // ch_count],
            send_sem=send_a.at[p],
            recv_sem=recv_a.at[src],
            device_id=(p // ch_count, lax.rem(p, ch_count)),
            device_id_type=MESH,
        )

    def copy_h(p, src):
        return pltpu.make_async_remote_copy(
            src_ref=txh.at[p * ch_count + c],
            dst_ref=rxh.at[src],
            send_sem=send_h.at[p],
            recv_sem=recv_h.at[src],
            device_id=(p, c),
            device_id_type=MESH,
        )

    def copy_o(p, src):
        return pltpu.make_async_remote_copy(
            src_ref=txo.at[lax.rem(p, ch_count), p // ch_count],
            dst_ref=rxo.at[src],
            send_sem=send_o.at[p],
            recv_sem=recv_o.at[src],
            device_id=(p // ch_count, lax.rem(p, ch_count)),
            device_id_type=MESH,
        )

    def copy_f(p, slot, target_c):
        return pltpu.make_async_remote_copy(
            src_ref=txf.at[p],
            dst_ref=rxf.at[slot],
            send_sem=send_f.at[p],
            recv_sem=recv_f.at[slot],
            device_id=(p, target_c),
            device_id_type=MESH,
        )

    pl.semaphore_wait(barrier, ndev - 1)

    def go(count, at, make):
        def step(i, _):
            make(lax.rem(at + i, count)).start()
            return 0

        lax.fori_loop(1, count, step, 0)

    def arrive(count, at, make):
        def step(i, _):
            make(lax.rem(at + count - i, count)).wait_recv()
            return 0

        lax.fori_loop(1, count, step, 0)

    def sent(count, at, make):
        def step(i, _):
            make(lax.rem(at + i, count)).wait_send()
            return 0

        lax.fori_loop(1, count, step, 0)

    go(seq_count, s, lambda p: copy_h(p, s))
    go(ndev, me, lambda p: copy_a(p, me))
    rx[c, s] = tx[me]
    rxh[s] = txh[me]

    tr, ti = twist[0], twist[1]

    def forward(a, lane):
        ar, ai = a[:rows, lane : lane + LANES], a[rows:, lane : lane + LANES]
        b = jnp.concatenate([ar * tr - ai * ti, ar * ti + ai * tr], axis=1)
        return right_table(b, second)

    def backward(y):
        y = right_table(y, second_t)
        yr, yi = y[:, :LANES], y[:, LANES:]
        return jnp.concatenate([yr * tr + yi * ti, yi * tr - yr * ti], axis=0)

    arrive(seq_count, s, lambda p: copy_h(p, p))
    spec = forward(left_table(first_taps, rxh[...].reshape(-1, LANES)), 0)
    kind = lax.rem(lax.broadcasted_iota(jnp.int32, (rows, LANES), 0), q) < nf
    hr = spec[:, :LANES]
    hi_ = jnp.where(kind, spec[:, LANES:], -spec[:, LANES:])

    arrive(ndev, me, lambda p: copy_a(p, p))
    filt_r = jnp.zeros((rows, LANES), f32)
    filt_i = jnp.zeros((rows, LANES), f32)
    for pair in range(0, ch_count, 2):
        x = jnp.concatenate(
            [rx[pair].reshape(rows, LANES), rx[pair + 1].reshape(rows, LANES)], axis=1
        )
        a = left_table(first, x)
        outs = []
        for half in range(2):
            z = forward(a, half * LANES)
            zr, zi = z[:, :LANES], z[:, LANES:]
            gr = pltpu.roll(zr, rows - nf, 0)
            gi = pltpu.roll(zi, rows - nf, 0)
            filt_r = filt_r + zr * gr + zi * gi
            filt_i = filt_i + zr * gi - zi * gr
            y = jnp.concatenate([hr * zr - hi_ * zi, hr * zi + hi_ * zr], axis=1)
            outs.append(backward(y))
        out = left_table(last, jnp.concatenate(outs, axis=1))
        txo[pair] = out[:, :LANES].reshape(txo.shape[1:])
        txo[pair + 1] = out[:, LANES:].reshape(txo.shape[1:])

    go(ndev, me, lambda p: copy_o(p, me))
    rxo[me] = txo[c, s]

    out = left_table(last_filt, backward(jnp.concatenate([filt_r, filt_i], axis=1)))
    txf[...] = out.reshape(txf.shape)
    slot, target_c = lax.rem(me, own), me // own

    go(seq_count, s, lambda p: copy_f(p, slot, target_c))

    @pl.when(target_c != c)
    def _():
        copy_f(s, slot, target_c).start()

    @pl.when(target_c == c)
    def _():
        rxf[slot] = txf[s]

    arrive(ndev, me, lambda p: copy_o(p, p))

    for j in range(nb):
        r = pl.ds(j * LANES, LANES)
        if perm.shape[0] == 1:
            got = rxo[:, j * q : (j + 1) * q, :].reshape(ndev * q, LANES)
        else:
            got = rxo[...].reshape(-1, LANES)
        hi, lo = split(got.T)
        table = perm[min(j, perm.shape[0] - 1)]
        got = mm(hi, table) + mm(lo, table)
        query, key = q_ref[r, :].astype(f32), k_ref[r, :].astype(f32)
        value, up = v_ref[r, :].astype(f32), u_ref[r, :].astype(f32)
        gain = gain_ref[...]
        pre = got[:, :filters] + gain * (key * value)
        back = got[:, filters:] + gain * (up * query)
        mix_ref[r, :] = (query * pre).astype(jnp.bfloat16)
        gq_ref[r, :] = (up * pre).astype(jnp.bfloat16)
        gk_ref[r, :] = (back * value).astype(jnp.bfloat16)
        gv_ref[r, :] = (back * key).astype(jnp.bfloat16)

    def filt_in(i, _):
        @pl.when(c * own + i != me)
        def _():
            copy_f(s, i, c).wait_recv()

        return 0

    lax.fori_loop(0, own, filt_in, 0)
    hi, lo = split(rxf[...].reshape(-1, LANES).T)
    for j in range(nb):
        got = mm(hi, sel[j]) + mm(lo, sel[j])
        gf_ref[pl.ds(j * LANES, LANES), :] = got[:, : gf_ref.shape[1]]

    sent(seq_count, s, lambda p: copy_h(p, s))
    sent(ndev, me, lambda p: copy_a(p, me))
    sent(ndev, me, lambda p: copy_o(p, me))
    sent(seq_count, s, lambda p: copy_f(p, slot, target_c))

    @pl.when(target_c != c)
    def _():
        copy_f(s, slot, target_c).wait_send()


def local(query_proj, key_proj, value_proj, filter_taps, skip_gain, grad_mixer):
    seq_count, ch_count = lax.axis_size("seq"), lax.axis_size("ch")
    ndev = seq_count * ch_count
    local_rows, filters = filter_taps.shape
    nb = local_rows // LANES
    nf = filters // ndev
    dup = max(1, 8 // (nb * nf))
    own = filters // ch_count // nf
    tabs = tables(seq_count, ch_count, nb, filters)
    ab, hb = nb * 2 * nf, nb * dup * nf
    f32, bf16 = jnp.float32, jnp.bfloat16
    vmem = pl.BlockSpec(memory_space=pltpu.VMEM)
    dma = pltpu.SemaphoreType.DMA
    wide = jax.ShapeDtypeStruct((local_rows, filters), bf16)
    return pl.pallas_call(
        functools.partial(kernel, seq_count, ch_count, nf),
        out_shape=(
            wide, wide, wide, wide,
            jax.ShapeDtypeStruct((local_rows, filters // ch_count), f32),
        ),
        in_specs=[vmem] * (6 + len(tabs)),
        out_specs=(vmem,) * 5,
        scratch_shapes=[
            pltpu.VMEM((ndev, ab, LANES), f32),
            pltpu.VMEM((ch_count, seq_count, ab, LANES), f32),
            pltpu.VMEM((ndev, hb, LANES), f32),
            pltpu.VMEM((seq_count, hb, LANES), f32),
            pltpu.VMEM((ch_count, seq_count, ab, LANES), f32),
            pltpu.VMEM((ndev, ab, LANES), f32),
            pltpu.VMEM((seq_count, hb, LANES), f32),
            pltpu.VMEM((own, hb, LANES), f32),
            dma((ndev,)), dma((ndev,)), dma((seq_count,)), dma((seq_count,)),
            dma((ndev,)), dma((ndev,)), dma((seq_count,)), dma((own,)),
        ],
        compiler_params=pltpu.CompilerParams(
            collective_id=0, has_side_effects=True, vmem_limit_bytes=48 * 2**20
        ),
    )(
        query_proj, key_proj, value_proj, filter_taps,
        skip_gain.reshape(1, filters), grad_mixer, *tabs,
    )


def solution(mesh):
    in_specs = (
        P("seq", "ch"),
        P("seq", "ch"),
        P("seq", "ch"),
        P("seq", None),
        P("ch"),
        P("seq", "ch"),
    )
    out_specs = (P("seq", "ch"), P("seq", "ch"), P("seq", "ch"), P("seq", "ch"), P("seq", "ch"))
    return jax.shard_map(local, mesh=mesh, in_specs=in_specs, out_specs=out_specs, check_vma=False)
```

```python
import functools
import math

import jax
import jax.numpy as jnp
import ml_dtypes
import numpy as np
from jax import lax
from jax.experimental import pallas as pl
from jax.experimental.pallas import tpu as pltpu
from jax.sharding import PartitionSpec as P

MESH = pl.DeviceIdType.MESH
LANES = 128


def halves(table):
    head = table.astype(np.float32).astype(ml_dtypes.bfloat16)
    tail = (table - head.astype(np.float64)).astype(np.float32).astype(ml_dtypes.bfloat16)
    return np.stack([head, tail])


@functools.lru_cache(maxsize=4)
def tables(seq_count, ch_count, nb, filters):
    ndev = seq_count * ch_count
    nf = filters // ndev
    dup = max(1, 8 // (nb * nf))
    n1 = seq_count * nb
    total = n1 * LANES
    a = np.arange(n1)
    ang = 2 * np.pi / n1 * ((a[:, None] + 0.25) * a[None, :])
    stack = np.concatenate([np.cos(ang), -np.sin(ang)], 0)
    first = np.kron(stack, np.eye(2 * nf))
    pick = np.kron(np.array([[1.0], [1.0]]), np.kron(np.eye(dup)[:1], np.eye(nf)))
    first_taps = np.kron(stack, pick)
    last = first.T / total
    keep = np.kron(np.ones((dup, 1)), np.concatenate([np.eye(nf), np.zeros((nf, nf))], 1))
    last_filt = np.kron(stack.T, keep) / total / math.sqrt(total)
    b = np.arange(LANES)
    turn = 2 * np.pi / total * ((a[:, None] + 0.25) * b[None, :])
    twist = np.repeat(np.stack([np.cos(turn), -np.sin(turn)]), 2 * nf, axis=1)
    ang2 = 2 * np.pi / LANES * (b[:, None] * b[None, :] % LANES)
    fr, fi = np.cos(ang2), -np.sin(ang2)
    second = np.block([[fr, fi], [-fi, fr]])
    d, kind, f = np.meshgrid(np.arange(ndev), np.arange(2), np.arange(nf), indexing="ij")
    perm = np.zeros((ndev, 2 * nf, 2 * filters))
    perm[d, kind * nf + f, kind * filters + d * nf + f] = 1.0
    if 2 * nf % 8:
        wide = np.zeros((nb, ndev, nb, 2 * nf, 2 * filters))
        for j in range(nb):
            wide[j, :, j] = perm
        perm = wide.reshape(nb, ndev * nb * 2 * nf, 2 * filters)
    else:
        perm = perm.reshape(1, ndev * 2 * nf, 2 * filters)
    perm_taps = np.zeros((nb, ndev, nb, dup, nf, filters))
    own = filters // ch_count // nf
    sel = np.zeros((nb, own, nb, dup, nf, LANES))
    for j in range(nb):
        for g in range(nf):
            for dev in range(ndev):
                perm_taps[j, dev, j, :, g, dev * nf + g] = 1.0
            for dev in range(own):
                sel[j, dev, j, 0, g, dev * nf + g] = 1.0
    bf = ml_dtypes.bfloat16
    perm_taps = perm_taps.reshape(nb, ndev * nb * dup * nf, filters).astype(bf)
    return (
        perm.astype(bf),
        perm_taps[:, :16, :] if len(perm) == 1 else perm_taps,
        halves(first),
        halves(first_taps),
        halves(last),
        halves(last_filt),
        halves(second),
        halves(second.T),
        twist.astype(np.float32),
        sel.reshape(nb, own * nb * dup * nf, LANES).astype(bf),
    )


def split(x):
    head = x.astype(jnp.bfloat16)
    return head, (x - head.astype(jnp.float32)).astype(jnp.bfloat16)


def mm(x, y):
    return jnp.dot(x, y, preferred_element_type=jnp.float32)


def mm_nt(x, y):
    return lax.dot_general(x, y, (((1,), (1,)), ((), ())), preferred_element_type=jnp.float32)


def left_table(table, x):
    hi, lo = split(x)
    return mm(table[0], hi) + mm(table[0], lo) + mm(table[1], hi)


def right_table(x, table):
    hi, lo = split(x)
    return mm(hi, table[0]) + mm(lo, table[0]) + mm(hi, table[1])


def kernel(
    seq_count, ch_count, nf,
    *refs,
):
    count = (len(refs) - 22) // 2
    stored, held = refs[:count], refs[count + 5 : 2 * count + 5]
    mix_ref, gq_ref, gk_ref, gv_ref, gf_ref = refs[count : count + 5]
    (
        tx, rx, txh, rxh, txo, rxo, txf, rxf,
        send_a, recv_a, send_h, recv_h, send_o, recv_o, send_f, recv_f, load_sem,
    ) = refs[2 * count + 5 :]
    q_ref, k_ref, v_ref, u_ref, h_ref, perm, perm_taps = held[:7]
    first, first_taps, last, last_filt, second, second_t, twist, sel, gain_ref = held[7:]
    loads = [
        pltpu.make_async_copy(src, dst, load_sem.at[i])
        for i, (src, dst) in enumerate(zip(stored, held))
    ]
    for load in loads:
        load.start()
    ndev = seq_count * ch_count
    local_rows, filters = h_ref.shape
    nb = local_rows // LANES
    q = 2 * nf
    own = rxf.shape[0]
    rows = seq_count * nb * q
    s, c = lax.axis_index("seq"), lax.axis_index("ch")
    me = s * ch_count + c
    f32 = jnp.float32

    barrier = pltpu.get_barrier_semaphore()

    def greet(i, _):
        p = lax.rem(me + i, ndev)
        pl.semaphore_signal(
            barrier, inc=1, device_id=(p // ch_count, lax.rem(p, ch_count)), device_id_type=MESH
        )
        return 0

    lax.fori_loop(1, ndev, greet, 0)

    for load in loads[:7]:
        load.wait()

    if perm.shape[0] == 1:
        for j in range(0, nb, 2):
            both = [h_ref[pl.ds((j + e) * LANES, LANES), :] for e in range(2)]
            hi, lo = split(jnp.concatenate(both, axis=1))
            part = mm_nt(perm[0], hi) + mm_nt(perm[0], lo)
            txh[:, j * nf : (j + 2) * nf, :] = part.reshape(ndev, q, LANES)
    else:
        acc = None
        for j in range(nb):
            hi, lo = split(h_ref[pl.ds(j * LANES, LANES), :])
            part = mm_nt(perm_taps[j], hi) + mm_nt(perm_taps[j], lo)
            acc = part if acc is None else acc + part
        txh[...] = acc.reshape(txh.shape)
    acc = None
    for j in range(nb):
        r = pl.ds(j * LANES, LANES)
        m = k_ref[r, :].astype(f32) * v_ref[r, :].astype(f32)
        g = u_ref[r, :].astype(f32) * q_ref[r, :].astype(f32)
        hi, lo = split(jnp.concatenate([m, g], axis=1))
        if perm.shape[0] == 1:
            part = mm_nt(perm[0], hi) + mm_nt(perm[0], lo)
            tx[:, j * q : (j + 1) * q, :] = part.reshape(ndev, q, LANES)
        else:
            part = mm_nt(perm[j], hi) + mm_nt(perm[j], lo)
            acc = part if acc is None else acc + part
    if acc is not None:
        tx[...] = acc.reshape(tx.shape)

    def copy_a(p, src):
        return pltpu.make_async_remote_copy(
            src_ref=tx.at[p],
            dst_ref=rx.at[lax.rem(src, ch_count), src // ch_count],
            send_sem=send_a.at[p],
            recv_sem=recv_a.at[src],
            device_id=(p // ch_count, lax.rem(p, ch_count)),
            device_id_type=MESH,
        )

    def copy_h(p, src):
        return pltpu.make_async_remote_copy(
            src_ref=txh.at[p * ch_count + c],
            dst_ref=rxh.at[src],
            send_sem=send_h.at[p],
            recv_sem=recv_h.at[src],
            device_id=(p, c),
            device_id_type=MESH,
        )

    def copy_o(p, src):
        return pltpu.make_async_remote_copy(
            src_ref=txo.at[lax.rem(p, ch_count), p // ch_count],
            dst_ref=rxo.at[src],
            send_sem=send_o.at[p],
            recv_sem=recv_o.at[src],
            device_id=(p // ch_count, lax.rem(p, ch_count)),
            device_id_type=MESH,
        )

    def copy_f(p, slot, target_c):
        return pltpu.make_async_remote_copy(
            src_ref=txf.at[p],
            dst_ref=rxf.at[slot],
            send_sem=send_f.at[p],
            recv_sem=recv_f.at[slot],
            device_id=(p, target_c),
            device_id_type=MESH,
        )

    pl.semaphore_wait(barrier, ndev - 1)

    def stride(count):
        return next(i for i in range(count * 2 // 5, count) if math.gcd(i, count) == 1)

    def go(count, at, make):
        def step(i, _):
            make(lax.rem(at + i * stride(count), count)).start()
            return 0

        lax.fori_loop(1, count, step, 0)

    def arrive(count, at, make):
        def step(i, _):
            make(lax.rem(at + count - i, count)).wait_recv()
            return 0

        lax.fori_loop(1, count, step, 0)

    def sent(count, at, make):
        def step(i, _):
            make(lax.rem(at + i, count)).wait_send()
            return 0

        lax.fori_loop(1, count, step, 0)

    go(seq_count, s, lambda p: copy_h(p, s))
    go(ndev, me, lambda p: copy_a(p, me))
    rx[c, s] = tx[me]
    rxh[s] = txh[me]

    for load in loads[7:]:
        load.wait()
    tr, ti = twist[0], twist[1]

    def forward(a, lane):
        ar, ai = a[:rows, lane : lane + LANES], a[rows:, lane : lane + LANES]
        b = jnp.concatenate([ar * tr - ai * ti, ar * ti + ai * tr], axis=1)
        return right_table(b, second)

    def backward(y):
        y = right_table(y, second_t)
        yr, yi = y[:, :LANES], y[:, LANES:]
        return jnp.concatenate([yr * tr + yi * ti, yi * tr - yr * ti], axis=0)

    arrive(seq_count, s, lambda p: copy_h(p, p))
    spec = forward(left_table(first_taps, rxh[...].reshape(-1, LANES)), 0)
    kind = lax.rem(lax.broadcasted_iota(jnp.int32, (rows, LANES), 0), q) < nf
    hr = spec[:, :LANES]
    hi_ = jnp.where(kind, spec[:, LANES:], -spec[:, LANES:])

    arrive(ndev, me, lambda p: copy_a(p, p))
    filt_r = jnp.zeros((rows, LANES), f32)
    filt_i = jnp.zeros((rows, LANES), f32)
    for pair in range(0, ch_count, 2):
        x = jnp.concatenate(
            [rx[pair].reshape(rows, LANES), rx[pair + 1].reshape(rows, LANES)], axis=1
        )
        a = left_table(first, x)
        outs = []
        for half in range(2):
            z = forward(a, half * LANES)
            zr, zi = z[:, :LANES], z[:, LANES:]
            gr = pltpu.roll(zr, rows - nf, 0)
            gi = pltpu.roll(zi, rows - nf, 0)
            filt_r = filt_r + zr * gr + zi * gi
            filt_i = filt_i + zr * gi - zi * gr
            y = jnp.concatenate([hr * zr - hi_ * zi, hr * zi + hi_ * zr], axis=1)
            outs.append(backward(y))
        out = left_table(last, jnp.concatenate(outs, axis=1))
        txo[pair] = out[:, :LANES].reshape(txo.shape[1:])
        txo[pair + 1] = out[:, LANES:].reshape(txo.shape[1:])

    go(ndev, me, lambda p: copy_o(p, me))
    rxo[me] = txo[c, s]

    out = left_table(last_filt, backward(jnp.concatenate([filt_r, filt_i], axis=1)))
    txf[...] = out.reshape(txf.shape)
    slot, target_c = lax.rem(me, own), me // own

    go(seq_count, s, lambda p: copy_f(p, slot, target_c))

    @pl.when(target_c != c)
    def _():
        copy_f(s, slot, target_c).start()

    @pl.when(target_c == c)
    def _():
        rxf[slot] = txf[s]

    arrive(ndev, me, lambda p: copy_o(p, p))

    for j in range(nb):
        r = pl.ds(j * LANES, LANES)
        if perm.shape[0] == 1:
            got = rxo[:, j * q : (j + 1) * q, :].reshape(ndev * q, LANES)
        else:
            got = rxo[...].reshape(-1, LANES)
        hi, lo = split(got.T)
        table = perm[min(j, perm.shape[0] - 1)]
        got = mm(hi, table) + mm(lo, table)
        query, key = q_ref[r, :].astype(f32), k_ref[r, :].astype(f32)
        value, up = v_ref[r, :].astype(f32), u_ref[r, :].astype(f32)
        gain = gain_ref[...]
        pre = got[:, :filters] + gain * (key * value)
        back = got[:, filters:] + gain * (up * query)
        mix_ref[r, :] = (query * pre).astype(jnp.bfloat16)
        gq_ref[r, :] = (up * pre).astype(jnp.bfloat16)
        gk_ref[r, :] = (back * value).astype(jnp.bfloat16)
        gv_ref[r, :] = (back * key).astype(jnp.bfloat16)

    def filt_in(i, _):
        @pl.when(c * own + i != me)
        def _():
            copy_f(s, i, c).wait_recv()

        return 0

    lax.fori_loop(0, own, filt_in, 0)
    hi, lo = split(rxf[...].reshape(-1, LANES).T)
    for j in range(nb):
        got = mm(hi, sel[j]) + mm(lo, sel[j])
        gf_ref[pl.ds(j * LANES, LANES), :] = got[:, : gf_ref.shape[1]]

    sent(seq_count, s, lambda p: copy_h(p, s))
    sent(ndev, me, lambda p: copy_a(p, me))
    sent(ndev, me, lambda p: copy_o(p, me))
    sent(seq_count, s, lambda p: copy_f(p, slot, target_c))

    @pl.when(target_c != c)
    def _():
        copy_f(s, slot, target_c).wait_send()


def local(query_proj, key_proj, value_proj, filter_taps, skip_gain, grad_mixer):
    seq_count, ch_count = lax.axis_size("seq"), lax.axis_size("ch")
    ndev = seq_count * ch_count
    local_rows, filters = filter_taps.shape
    nb = local_rows // LANES
    nf = filters // ndev
    dup = max(1, 8 // (nb * nf))
    own = filters // ch_count // nf
    tabs = tables(seq_count, ch_count, nb, filters)
    ab, hb = nb * 2 * nf, nb * dup * nf
    f32, bf16 = jnp.float32, jnp.bfloat16
    vmem = pl.BlockSpec(memory_space=pltpu.VMEM)
    dma = pltpu.SemaphoreType.DMA
    wide = jax.ShapeDtypeStruct((local_rows, filters), bf16)
    operands = (
        query_proj, key_proj, value_proj, grad_mixer, filter_taps, *tabs,
        skip_gain.reshape(1, filters),
    )
    return pl.pallas_call(
        functools.partial(kernel, seq_count, ch_count, nf),
        out_shape=(
            wide, wide, wide, wide,
            jax.ShapeDtypeStruct((local_rows, filters // ch_count), f32),
        ),
        in_specs=[pl.BlockSpec(memory_space=pltpu.HBM)] * len(operands),
        out_specs=(vmem,) * 5,
        scratch_shapes=[pltpu.VMEM(x.shape, x.dtype) for x in operands]
        + [
            pltpu.VMEM((ndev, ab, LANES), f32),
            pltpu.VMEM((ch_count, seq_count, ab, LANES), f32),
            pltpu.VMEM((ndev, hb, LANES), f32),
            pltpu.VMEM((seq_count, hb, LANES), f32),
            pltpu.VMEM((ch_count, seq_count, ab, LANES), f32),
            pltpu.VMEM((ndev, ab, LANES), f32),
            pltpu.VMEM((seq_count, hb, LANES), f32),
            pltpu.VMEM((own, hb, LANES), f32),
            dma((ndev,)), dma((ndev,)), dma((seq_count,)), dma((seq_count,)),
            dma((ndev,)), dma((ndev,)), dma((seq_count,)), dma((own,)),
            dma((len(operands),)),
        ],
        compiler_params=pltpu.CompilerParams(
            collective_id=0, has_side_effects=True, vmem_limit_bytes=48 * 2**20
        ),
    )(*operands)


def solution(mesh):
    in_specs = (
        P("seq", "ch"),
        P("seq", "ch"),
        P("seq", "ch"),
        P("seq", None),
        P("ch"),
        P("seq", "ch"),
    )
    out_specs = (P("seq", "ch"), P("seq", "ch"), P("seq", "ch"), P("seq", "ch"), P("seq", "ch"))
    return jax.shard_map(local, mesh=mesh, in_specs=in_specs, out_specs=out_specs, check_vma=False)
```

```python
import functools
import math

import jax
import jax.numpy as jnp
import ml_dtypes
import numpy as np
from jax import lax
from jax.experimental import pallas as pl
from jax.experimental.pallas import tpu as pltpu
from jax.sharding import PartitionSpec as P

MESH = pl.DeviceIdType.MESH
LANES = 128
VMEM_BYTES = 64 * 2**20


def halves(table):
    head = table.astype(np.float32).astype(ml_dtypes.bfloat16)
    tail = (table - head.astype(np.float64)).astype(np.float32).astype(ml_dtypes.bfloat16)
    return np.stack([head, tail])


@functools.lru_cache(maxsize=4)
def tables(seq_count, ch_count, nb, filters):
    ndev = seq_count * ch_count
    nf = filters // ndev
    dup = max(1, 8 // (nb * nf))
    n1 = seq_count * nb
    total = n1 * LANES
    a = np.arange(n1)
    ang = 2 * np.pi / n1 * ((a[:, None] + 0.25) * a[None, :])
    stack = np.concatenate([np.cos(ang), -np.sin(ang)], 0)
    first = np.kron(stack, np.eye(2 * nf))
    pick = np.kron(np.array([[1.0], [1.0]]), np.kron(np.eye(dup)[:1], np.eye(nf)))
    first_taps = np.kron(stack, pick)
    last = first.T / total
    keep = np.kron(np.ones((dup, 1)), np.concatenate([np.eye(nf), np.zeros((nf, nf))], 1))
    last_filt = np.kron(stack.T, keep) / total / math.sqrt(total)
    b = np.arange(LANES)
    turn = 2 * np.pi / total * ((a[:, None] + 0.25) * b[None, :])
    twist = np.repeat(np.stack([np.cos(turn), -np.sin(turn)]), 2 * nf, axis=1)
    ang2 = 2 * np.pi / LANES * (b[:, None] * b[None, :] % LANES)
    fr, fi = np.cos(ang2), -np.sin(ang2)
    second = np.block([[fr, fi], [-fi, fr]])
    d, kind, f = np.meshgrid(np.arange(ndev), np.arange(2), np.arange(nf), indexing="ij")
    perm = np.zeros((ndev, 2 * nf, 2 * filters))
    perm[d, kind * nf + f, kind * filters + d * nf + f] = 1.0
    if 2 * nf % 8:
        wide = np.zeros((nb, ndev, nb, 2 * nf, 2 * filters))
        for j in range(nb):
            wide[j, :, j] = perm
        perm = wide.reshape(nb, ndev * nb * 2 * nf, 2 * filters)
    else:
        perm = perm.reshape(1, ndev * 2 * nf, 2 * filters)
    perm_taps = np.zeros((nb, ndev, nb, dup, nf, filters))
    own = filters // ch_count // nf
    sel = np.zeros((nb, own * nf, own, nb, dup, nf))
    for j in range(nb):
        for g in range(nf):
            for dev in range(ndev):
                perm_taps[j, dev, j, :, g, dev * nf + g] = 1.0
            for dev in range(own):
                sel[j, dev * nf + g, dev, j, 0, g] = 1.0
    bf = ml_dtypes.bfloat16
    perm_taps = perm_taps.reshape(nb, ndev * nb * dup * nf, filters).astype(bf)
    return (
        perm.astype(bf),
        perm_taps[:, :16, :] if len(perm) == 1 else perm_taps,
        halves(first),
        halves(first_taps),
        halves(last),
        halves(last_filt),
        halves(second),
        halves(second.T),
        twist.astype(np.float32),
    ), sel.reshape(nb, own * nf, own * nb * dup * nf).astype(bf)


def split(x):
    head = x.astype(jnp.bfloat16)
    return head, (x - head.astype(jnp.float32)).astype(jnp.bfloat16)


def mm(x, y):
    return jnp.dot(x, y, preferred_element_type=jnp.float32)


def mm_nt(x, y):
    return lax.dot_general(x, y, (((1,), (1,)), ((), ())), preferred_element_type=jnp.float32)


def left_table(table, x):
    hi, lo = split(x)
    return mm(table[0], hi) + mm(table[0], lo) + mm(table[1], hi)


def right_table(x, table):
    hi, lo = split(x)
    return mm(hi, table[0]) + mm(lo, table[0]) + mm(hi, table[1])


def kernel(
    seq_count, ch_count, nf,
    *refs,
):
    count = (len(refs) - 18) // 2
    stored, held = refs[:count], refs[count + 2 : 2 * count + 2]
    rxo, rxf = refs[count : count + 2]
    (
        tx, rx, txh, rxh, txo, txf,
        send_a, recv_a, send_h, recv_h, send_o, recv_o, send_f, recv_f, load_sem, own_sem,
    ) = refs[2 * count + 2 :]
    q_ref, k_ref, v_ref, u_ref, h_ref, perm, perm_taps = held[:7]
    first, first_taps, last, last_filt, second, second_t, twist = held[7:]
    loads = [
        pltpu.make_async_copy(src, dst, load_sem.at[i])
        for i, (src, dst) in enumerate(zip(stored, held))
    ]
    for load in loads:
        load.start()
    ndev = seq_count * ch_count
    local_rows, filters = h_ref.shape
    nb = local_rows // LANES
    q = 2 * nf
    own = rxf.shape[0]
    rows = seq_count * nb * q
    s, c = lax.axis_index("seq"), lax.axis_index("ch")
    me = s * ch_count + c
    f32 = jnp.float32

    barrier = pltpu.get_barrier_semaphore()

    def greet(i, _):
        p = lax.rem(me + i, ndev)
        pl.semaphore_signal(
            barrier, inc=1, device_id=(p // ch_count, lax.rem(p, ch_count)), device_id_type=MESH
        )
        return 0

    lax.fori_loop(1, ndev, greet, 0)

    for load in loads[:7]:
        load.wait()

    if perm.shape[0] == 1:
        for j in range(0, nb, 2):
            both = [h_ref[pl.ds((j + e) * LANES, LANES), :] for e in range(2)]
            hi, lo = split(jnp.concatenate(both, axis=1))
            part = mm_nt(perm[0], hi) + mm_nt(perm[0], lo)
            txh[:, j * nf : (j + 2) * nf, :] = part.reshape(ndev, q, LANES)
    else:
        acc = None
        for j in range(nb):
            hi, lo = split(h_ref[pl.ds(j * LANES, LANES), :])
            part = mm_nt(perm_taps[j], hi) + mm_nt(perm_taps[j], lo)
            acc = part if acc is None else acc + part
        txh[...] = acc.reshape(txh.shape)
    acc = None
    for j in range(nb):
        r = pl.ds(j * LANES, LANES)
        m = k_ref[r, :].astype(f32) * v_ref[r, :].astype(f32)
        g = u_ref[r, :].astype(f32) * q_ref[r, :].astype(f32)
        hi, lo = split(jnp.concatenate([m, g], axis=1))
        if perm.shape[0] == 1:
            part = mm_nt(perm[0], hi) + mm_nt(perm[0], lo)
            tx[:, j * q : (j + 1) * q, :] = part.reshape(ndev, q, LANES)
        else:
            part = mm_nt(perm[j], hi) + mm_nt(perm[j], lo)
            acc = part if acc is None else acc + part
    if acc is not None:
        tx[...] = acc.reshape(tx.shape)

    def copy_a(p, src):
        return pltpu.make_async_remote_copy(
            src_ref=tx.at[p],
            dst_ref=rx.at[lax.rem(src, ch_count), src // ch_count],
            send_sem=send_a.at[p],
            recv_sem=recv_a.at[src],
            device_id=(p // ch_count, lax.rem(p, ch_count)),
            device_id_type=MESH,
        )

    def copy_h(p, src):
        return pltpu.make_async_remote_copy(
            src_ref=txh.at[p * ch_count + c],
            dst_ref=rxh.at[src],
            send_sem=send_h.at[p],
            recv_sem=recv_h.at[src],
            device_id=(p, c),
            device_id_type=MESH,
        )

    def copy_o(p, src):
        return pltpu.make_async_remote_copy(
            src_ref=txo.at[lax.rem(p, ch_count), p // ch_count],
            dst_ref=rxo.at[src],
            send_sem=send_o.at[p],
            recv_sem=recv_o.at[src],
            device_id=(p // ch_count, lax.rem(p, ch_count)),
            device_id_type=MESH,
        )

    def copy_f(p, slot, target_c):
        return pltpu.make_async_remote_copy(
            src_ref=txf.at[p],
            dst_ref=rxf.at[slot],
            send_sem=send_f.at[p],
            recv_sem=recv_f.at[slot],
            device_id=(p, target_c),
            device_id_type=MESH,
        )

    pl.semaphore_wait(barrier, ndev - 1)

    def go(count, at, make):
        def step(i, _):
            make(lax.rem(at + i, count)).start()
            return 0

        lax.fori_loop(1, count, step, 0)

    def arrive(count, at, make):
        def step(i, _):
            make(lax.rem(at + count - i, count)).wait_recv()
            return 0

        lax.fori_loop(1, count, step, 0)

    def sent(count, at, make):
        def step(i, _):
            make(lax.rem(at + i, count)).wait_send()
            return 0

        lax.fori_loop(1, count, step, 0)

    go(seq_count, s, lambda p: copy_h(p, s))
    go(ndev, me, lambda p: copy_a(p, me))
    rx[c, s] = tx[me]
    rxh[s] = txh[me]

    for load in loads[7:]:
        load.wait()
    tr, ti = twist[0], twist[1]

    def forward(a, lane):
        ar, ai = a[:rows, lane : lane + LANES], a[rows:, lane : lane + LANES]
        b = jnp.concatenate([ar * tr - ai * ti, ar * ti + ai * tr], axis=1)
        return right_table(b, second)

    def backward(y):
        y = right_table(y, second_t)
        yr, yi = y[:, :LANES], y[:, LANES:]
        return jnp.concatenate([yr * tr + yi * ti, yi * tr - yr * ti], axis=0)

    arrive(seq_count, s, lambda p: copy_h(p, p))
    spec = forward(left_table(first_taps, rxh[...].reshape(-1, LANES)), 0)
    kind = lax.rem(lax.broadcasted_iota(jnp.int32, (rows, LANES), 0), q) < nf
    hr = spec[:, :LANES]
    hi_ = jnp.where(kind, spec[:, LANES:], -spec[:, LANES:])

    arrive(ndev, me, lambda p: copy_a(p, p))
    filt_r = jnp.zeros((rows, LANES), f32)
    filt_i = jnp.zeros((rows, LANES), f32)
    for pair in range(0, ch_count, 2):
        x = jnp.concatenate(
            [rx[pair].reshape(rows, LANES), rx[pair + 1].reshape(rows, LANES)], axis=1
        )
        a = left_table(first, x)
        outs = []
        for half in range(2):
            z = forward(a, half * LANES)
            zr, zi = z[:, :LANES], z[:, LANES:]
            gr = pltpu.roll(zr, rows - nf, 0)
            gi = pltpu.roll(zi, rows - nf, 0)
            filt_r = filt_r + zr * gr + zi * gi
            filt_i = filt_i + zr * gi - zi * gr
            y = jnp.concatenate([hr * zr - hi_ * zi, hr * zi + hi_ * zr], axis=1)
            outs.append(backward(y))
        out = left_table(last, jnp.concatenate(outs, axis=1))
        txo[pair] = out[:, :LANES].reshape(txo.shape[1:])
        txo[pair + 1] = out[:, LANES:].reshape(txo.shape[1:])

    go(ndev, me, lambda p: copy_o(p, me))
    own_o = pltpu.make_async_copy(txo.at[c, s], rxo.at[me], own_sem.at[0])
    own_o.start()

    out = left_table(last_filt, backward(jnp.concatenate([filt_r, filt_i], axis=1)))
    txf[...] = out.reshape(txf.shape)
    slot, target_c = lax.rem(me, own), me // own

    go(seq_count, s, lambda p: copy_f(p, slot, target_c))

    @pl.when(target_c != c)
    def _():
        copy_f(s, slot, target_c).start()

    @pl.when(target_c == c)
    def _():
        pltpu.make_async_copy(txf.at[s], rxf.at[slot], own_sem.at[1]).start()

    arrive(ndev, me, lambda p: copy_o(p, p))

    def filt_in(i, _):
        @pl.when(c * own + i != me)
        def _():
            copy_f(s, i, c).wait_recv()

        return 0

    lax.fori_loop(0, own, filt_in, 0)
    sent(seq_count, s, lambda p: copy_h(p, s))
    sent(ndev, me, lambda p: copy_a(p, me))
    sent(ndev, me, lambda p: copy_o(p, me))
    sent(seq_count, s, lambda p: copy_f(p, slot, target_c))

    @pl.when(target_c != c)
    def _():
        copy_f(s, slot, target_c).wait_send()

    @pl.when(target_c == c)
    def _():
        pltpu.make_async_copy(txf.at[s], rxf.at[slot], own_sem.at[1]).wait()

    own_o.wait()


def finish(nf, *refs):
    stored, drained = refs[:9], refs[9:14]
    held, made = refs[14:23], refs[23:28]
    load_sem, store_sem = refs[28:]
    loads = [
        pltpu.make_async_copy(src, dst, load_sem.at[i])
        for i, (src, dst) in enumerate(zip(stored, held))
    ]
    for load in loads:
        load.start()
    stores = [
        pltpu.make_async_copy(src, dst, store_sem.at[i])
        for i, (src, dst) in enumerate(zip(made, drained))
    ]
    rxo, perm, q_ref, k_ref, v_ref, u_ref, gain_ref, rxf, sel = held
    mix_ref, gq_ref, gk_ref, gv_ref, gf_ref = made
    local_rows, filters = q_ref.shape
    nb = local_rows // LANES
    q = 2 * nf
    ndev = rxo.shape[0]
    f32 = jnp.float32
    for load in loads:
        load.wait()
    hi, lo = split(rxf[...].reshape(-1, LANES))
    for j in range(nb):
        gf_ref[:, j * LANES : (j + 1) * LANES] = mm(sel[j], hi) + mm(sel[j], lo)
    stores[4].start()
    for j in range(nb):
        r = pl.ds(j * LANES, LANES)
        if perm.shape[0] == 1:
            got = rxo[:, j * q : (j + 1) * q, :].reshape(ndev * q, LANES)
        else:
            got = rxo[...].reshape(-1, LANES)
        hi, lo = split(got.T)
        table = perm[min(j, perm.shape[0] - 1)]
        got = mm(hi, table) + mm(lo, table)
        query, key = q_ref[r, :].astype(f32), k_ref[r, :].astype(f32)
        value, up = v_ref[r, :].astype(f32), u_ref[r, :].astype(f32)
        gain = gain_ref[...]
        pre = got[:, :filters] + gain * (key * value)
        back = got[:, filters:] + gain * (up * query)
        mix_ref[r, :] = (query * pre).astype(jnp.bfloat16)
        gq_ref[r, :] = (up * pre).astype(jnp.bfloat16)
        gk_ref[r, :] = (back * value).astype(jnp.bfloat16)
        gv_ref[r, :] = (back * key).astype(jnp.bfloat16)
    for store in stores[:4]:
        store.start()
    for store in stores:
        store.wait()


def local(query_proj, key_proj, value_proj, filter_taps, skip_gain, grad_mixer):
    seq_count, ch_count = lax.axis_size("seq"), lax.axis_size("ch")
    ndev = seq_count * ch_count
    local_rows, filters = filter_taps.shape
    nb = local_rows // LANES
    nf = filters // ndev
    dup = max(1, 8 // (nb * nf))
    own = filters // ch_count // nf
    tabs, sel = tables(seq_count, ch_count, nb, filters)
    ab, hb = nb * 2 * nf, nb * dup * nf
    f32, bf16 = jnp.float32, jnp.bfloat16
    hbm = pl.BlockSpec(memory_space=pltpu.HBM)
    dma = pltpu.SemaphoreType.DMA
    operands = (query_proj, key_proj, value_proj, grad_mixer, filter_taps, *tabs)
    home, filt = pl.pallas_call(
        functools.partial(kernel, seq_count, ch_count, nf),
        out_shape=(
            jax.ShapeDtypeStruct((ndev, ab, LANES), f32),
            jax.ShapeDtypeStruct((own, hb, LANES), f32),
        ),
        in_specs=[hbm] * len(operands),
        out_specs=(hbm,) * 2,
        scratch_shapes=[pltpu.VMEM(x.shape, x.dtype) for x in operands]
        + [
            pltpu.VMEM((ndev, ab, LANES), f32),
            pltpu.VMEM((ch_count, seq_count, ab, LANES), f32),
            pltpu.VMEM((ndev, hb, LANES), f32),
            pltpu.VMEM((seq_count, hb, LANES), f32),
            pltpu.VMEM((ch_count, seq_count, ab, LANES), f32),
            pltpu.VMEM((seq_count, hb, LANES), f32),
            dma((ndev,)), dma((ndev,)), dma((seq_count,)), dma((seq_count,)),
            dma((ndev,)), dma((ndev,)), dma((seq_count,)), dma((own,)),
            dma((len(operands),)), dma((2,)),
        ],
        compiler_params=pltpu.CompilerParams(
            collective_id=0, has_side_effects=True, vmem_limit_bytes=VMEM_BYTES
        ),
    )(*operands)
    wide = jax.ShapeDtypeStruct((local_rows, filters), bf16)
    results = (wide, wide, wide, wide, jax.ShapeDtypeStruct((own * nf, local_rows), f32))
    operands = (
        home, tabs[0], query_proj, key_proj, value_proj, grad_mixer,
        skip_gain.reshape(1, filters), filt, sel,
    )
    *outs, grad_filter = pl.pallas_call(
        functools.partial(finish, nf),
        out_shape=results,
        in_specs=[hbm] * len(operands),
        out_specs=(hbm,) * 5,
        scratch_shapes=[pltpu.VMEM(x.shape, x.dtype) for x in operands + results]
        + [dma((len(operands),)), dma((5,))],
        compiler_params=pltpu.CompilerParams(vmem_limit_bytes=VMEM_BYTES),
    )(*operands)
    return (*outs, grad_filter.T)


def solution(mesh):
    in_specs = (
        P("seq", "ch"),
        P("seq", "ch"),
        P("seq", "ch"),
        P("seq", None),
        P("ch"),
        P("seq", "ch"),
    )
    out_specs = (P("seq", "ch"), P("seq", "ch"), P("seq", "ch"), P("seq", "ch"), P("seq", "ch"))
    return jax.shard_map(local, mesh=mesh, in_specs=in_specs, out_specs=out_specs, check_vma=False)
```

```python
import functools
import math

import jax
import jax.numpy as jnp
import ml_dtypes
import numpy as np
from jax import lax
from jax.experimental import pallas as pl
from jax.experimental.pallas import tpu as pltpu
from jax.sharding import PartitionSpec as P

MESH = pl.DeviceIdType.MESH
LANES = 128
VMEM_BYTES = 64 * 2**20


def chunking(nf):
    chunks = 2 if nf % 4 == 0 else 1
    return chunks, nf // chunks


def halves(table):
    head = table.astype(np.float32).astype(ml_dtypes.bfloat16)
    tail = (table - head.astype(np.float64)).astype(np.float32).astype(ml_dtypes.bfloat16)
    return np.stack([head, tail])


@functools.lru_cache(maxsize=4)
def tables(seq_count, ch_count, nb, filters):
    ndev = seq_count * ch_count
    nf = filters // ndev
    dup = max(1, 8 // (nb * nf))
    n1 = seq_count * nb
    total = n1 * LANES
    a = np.arange(n1)
    ang = 2 * np.pi / n1 * ((a[:, None] + 0.25) * a[None, :])
    stack = np.concatenate([np.cos(ang), -np.sin(ang)], 0)
    chunks, part = chunking(nf)
    first = np.kron(stack, np.eye(2 * part))
    last = first.T / total
    stack = stack.reshape(2, n1, n1)
    owner = np.eye(nf).reshape(chunks, part, nf)
    one = np.eye(dup)[0]
    first_taps = np.einsum("rkn,bpf,q,d->rbkqpndf", stack, owner, np.ones(2), one)
    first_taps = first_taps.reshape(2 * chunks * n1 * 2 * part, n1 * dup * nf)
    last_filt = np.einsum("rkn,bpf,q,d->ndfrbkqp", stack, owner, np.eye(2)[0], np.ones(dup))
    last_filt = last_filt.reshape(n1 * dup * nf, -1) / total / math.sqrt(total)
    b = np.arange(LANES)
    turn = 2 * np.pi / total * ((a[:, None] + 0.25) * b[None, :])
    twist = np.repeat(np.stack([np.cos(turn), -np.sin(turn)]), 2 * part, axis=1)
    ang2 = 2 * np.pi / LANES * (b[:, None] * b[None, :] % LANES)
    fr, fi = np.cos(ang2), -np.sin(ang2)
    second = np.block([[fr, fi], [-fi, fr]])
    place = np.eye(filters).reshape(ndev, chunks, part, filters)
    group = max(1, 8 // (2 * part))
    perm = np.einsum("dbpc,ij,kl->bdikpjlc", place, np.eye(group), np.eye(2))
    perm = perm.reshape(chunks * ndev * group * 2 * part, group * 2 * filters)
    group = max(1, 8 // (nf * dup))
    place = np.eye(filters).reshape(ndev, nf, filters)
    perm_taps = np.einsum("dfc,ij,e->diefjc", place, np.eye(group), np.ones(dup))
    perm_taps = perm_taps.reshape(ndev * group * dup * nf, group * filters)
    own = filters // ch_count // nf
    sel = np.zeros((nb, own * nf, own, nb, dup, nf))
    for j in range(nb):
        for g in range(nf):
            for dev in range(own):
                sel[j, dev * nf + g, dev, j, 0, g] = 1.0
    bf = ml_dtypes.bfloat16
    return (
        perm.astype(bf),
        perm_taps.astype(bf),
        halves(first),
        halves(first_taps),
        halves(last),
        halves(last_filt),
        halves(second),
        halves(second.T),
        twist.astype(np.float32),
    ), sel.reshape(nb, own * nf, own * nb * dup * nf).astype(bf)


def split(x):
    head = x.astype(jnp.bfloat16)
    return head, (x - head.astype(jnp.float32)).astype(jnp.bfloat16)


def mm(x, y):
    return jnp.dot(x, y, preferred_element_type=jnp.float32)


def mm_nt(x, y):
    return lax.dot_general(x, y, (((1,), (1,)), ((), ())), preferred_element_type=jnp.float32)


def left_table(table, x):
    hi, lo = split(x)
    return mm(table[0], hi) + mm(table[0], lo) + mm(table[1], hi)


def right_table(x, table):
    hi, lo = split(x)
    return mm(hi, table[0]) + mm(lo, table[0]) + mm(hi, table[1])


def kernel(
    seq_count, ch_count, nf,
    *refs,
):
    count = (len(refs) - 18) // 2
    stored, held = refs[:count], refs[count + 2 : 2 * count + 2]
    rxo, rxf = refs[count : count + 2]
    (
        tx, rx, txh, rxh, txo, txf,
        send_a, recv_a, send_h, recv_h, send_o, recv_o, send_f, recv_f, load_sem, own_sem,
    ) = refs[2 * count + 2 :]
    q_ref, k_ref, v_ref, u_ref, h_ref, perm, perm_taps = held[:7]
    first, first_taps, last, last_filt, second, second_t, twist = held[7:]
    loads = [
        pltpu.make_async_copy(src, dst, load_sem.at[i])
        for i, (src, dst) in enumerate(zip(stored, held))
    ]
    for load in loads:
        load.start()
    ndev = seq_count * ch_count
    local_rows, filters = h_ref.shape
    nb = local_rows // LANES
    chunks, part = chunking(nf)
    q = 2 * part
    own = rxf.shape[0]
    rows = seq_count * nb * q
    s, c = lax.axis_index("seq"), lax.axis_index("ch")
    me = s * ch_count + c
    f32 = jnp.float32

    barrier = pltpu.get_barrier_semaphore()

    def greet(i, _):
        p = lax.rem(me + i, ndev)
        pl.semaphore_signal(
            barrier, inc=1, device_id=(p // ch_count, lax.rem(p, ch_count)), device_id_type=MESH
        )
        return 0

    lax.fori_loop(1, ndev, greet, 0)

    for load in loads[:7]:
        load.wait()

    def turn(table, blocks):
        hi, lo = split(jnp.concatenate(blocks, axis=1))
        return mm_nt(table[...], hi) + mm_nt(table[...], lo)

    width = perm_taps.shape[1] // filters
    for j in range(0, nb, width):
        out = turn(perm_taps, [h_ref[pl.ds((j + e) * LANES, LANES), :] for e in range(width)])
        at = j // width * 8
        txh[:, at : at + 8, :] = out.reshape(ndev, 8, LANES)

    def send_products():
        width = perm.shape[1] // (2 * filters)
        for j in range(0, nb, width):
            blocks = []
            for e in range(width):
                r = pl.ds((j + e) * LANES, LANES)
                blocks.append(k_ref[r, :].astype(f32) * v_ref[r, :].astype(f32))
                blocks.append(u_ref[r, :].astype(f32) * q_ref[r, :].astype(f32))
            at = j // width * 8
            tx[:, :, at : at + 8, :] = turn(perm, blocks).reshape(chunks, ndev, 8, LANES)

    send_products()

    def copy_a(b, p, src):
        return pltpu.make_async_remote_copy(
            src_ref=tx.at[b, p],
            dst_ref=rx.at[b, lax.rem(src, ch_count), src // ch_count],
            send_sem=send_a.at[b, p],
            recv_sem=recv_a.at[b, src],
            device_id=(p // ch_count, lax.rem(p, ch_count)),
            device_id_type=MESH,
        )

    def copy_h(p, src):
        return pltpu.make_async_remote_copy(
            src_ref=txh.at[p * ch_count + c],
            dst_ref=rxh.at[src],
            send_sem=send_h.at[p],
            recv_sem=recv_h.at[src],
            device_id=(p, c),
            device_id_type=MESH,
        )

    def copy_o(b, p, src):
        return pltpu.make_async_remote_copy(
            src_ref=txo.at[b, lax.rem(p, ch_count), p // ch_count],
            dst_ref=rxo.at[b, src],
            send_sem=send_o.at[b, p],
            recv_sem=recv_o.at[b, src],
            device_id=(p // ch_count, lax.rem(p, ch_count)),
            device_id_type=MESH,
        )

    def copy_f(p, slot, target_c):
        return pltpu.make_async_remote_copy(
            src_ref=txf.at[p],
            dst_ref=rxf.at[slot],
            send_sem=send_f.at[p],
            recv_sem=recv_f.at[slot],
            device_id=(p, target_c),
            device_id_type=MESH,
        )

    pl.semaphore_wait(barrier, ndev - 1)

    def go(count, at, make):
        def step(i, _):
            make(lax.rem(at + i, count)).start()
            return 0

        lax.fori_loop(1, count, step, 0)

    def arrive(count, at, make):
        def step(i, _):
            make(lax.rem(at + count - i, count)).wait_recv()
            return 0

        lax.fori_loop(1, count, step, 0)

    def sent(count, at, make):
        def step(i, _):
            make(lax.rem(at + i, count)).wait_send()
            return 0

        lax.fori_loop(1, count, step, 0)

    go(seq_count, s, lambda p: copy_h(p, s))
    for b in range(chunks):
        go(ndev, me, lambda p: copy_a(b, p, me))
        rx[b, c, s] = tx[b, me]
    rxh[s] = txh[me]

    for load in loads[7:]:
        load.wait()
    tr, ti = twist[0], twist[1]

    def forward(ar, ai, times):
        tr2, ti2 = jnp.concatenate([tr] * times, axis=0), jnp.concatenate([ti] * times, axis=0)
        b = jnp.concatenate([ar * tr2 - ai * ti2, ar * ti2 + ai * tr2], axis=1)
        z = right_table(b, second)
        return z[:, :LANES], z[:, LANES:]

    def backward(yr, yi, times):
        tr2, ti2 = jnp.concatenate([tr] * times, axis=0), jnp.concatenate([ti] * times, axis=0)
        y = right_table(jnp.concatenate([yr, yi], axis=1), second_t)
        yr, yi = y[:, :LANES], y[:, LANES:]
        return yr * tr2 + yi * ti2, yi * tr2 - yr * ti2

    arrive(seq_count, s, lambda p: copy_h(p, p))
    a = left_table(first_taps, rxh[...].reshape(-1, LANES))
    taps_r, taps_i = forward(a[: chunks * rows], a[chunks * rows :], chunks)
    kind = lax.rem(lax.broadcasted_iota(jnp.int32, (chunks * rows, LANES), 0), q) < part
    taps_i = jnp.where(kind, taps_i, -taps_i)

    filts_r, filts_i, own_o = [], [], []
    for b in range(chunks):
        arrive(ndev, me, lambda p: copy_a(b, p, p))
        hr, hi_ = taps_r[b * rows : (b + 1) * rows], taps_i[b * rows : (b + 1) * rows]
        hr, hi_ = jnp.concatenate([hr, hr], axis=0), jnp.concatenate([hi_, hi_], axis=0)
        filt_r = jnp.zeros((rows, LANES), f32)
        filt_i = jnp.zeros((rows, LANES), f32)
        for pair in range(0, ch_count, 2):
            x = jnp.concatenate(
                [rx[b, pair].reshape(rows, LANES), rx[b, pair + 1].reshape(rows, LANES)], axis=1
            )
            a = left_table(first, x)
            zr, zi = forward(
                jnp.concatenate([a[:rows, :LANES], a[:rows, LANES:]], axis=0),
                jnp.concatenate([a[rows:, :LANES], a[rows:, LANES:]], axis=0),
                2,
            )
            gr = pltpu.roll(zr, 2 * rows - part, 0)
            gi = pltpu.roll(zi, 2 * rows - part, 0)
            cr, ci = zr * gr + zi * gi, zr * gi - zi * gr
            filt_r = filt_r + cr[:rows] + cr[rows:]
            filt_i = filt_i + ci[:rows] + ci[rows:]
            dr, di = backward(hr * zr - hi_ * zi, hr * zi + hi_ * zr, 2)
            d = jnp.concatenate(
                [
                    jnp.concatenate([dr[:rows], dr[rows:]], axis=1),
                    jnp.concatenate([di[:rows], di[rows:]], axis=1),
                ],
                axis=0,
            )
            out = left_table(last, d)
            txo[b, pair] = out[:, :LANES].reshape(txo.shape[2:])
            txo[b, pair + 1] = out[:, LANES:].reshape(txo.shape[2:])
        filts_r.append(filt_r)
        filts_i.append(filt_i)
        go(ndev, me, lambda p: copy_o(b, p, me))
        keep = pltpu.make_async_copy(txo.at[b, c, s], rxo.at[b, me], own_sem.at[b + 1])
        keep.start()
        own_o.append(keep)

    dr, di = backward(
        jnp.concatenate(filts_r, axis=0), jnp.concatenate(filts_i, axis=0), chunks
    )
    out = left_table(last_filt, jnp.concatenate([dr, di], axis=0))
    txf[...] = out.reshape(txf.shape)
    slot, target_c = lax.rem(me, own), me // own

    go(seq_count, s, lambda p: copy_f(p, slot, target_c))

    @pl.when(target_c != c)
    def _():
        copy_f(s, slot, target_c).start()

    @pl.when(target_c == c)
    def _():
        pltpu.make_async_copy(txf.at[s], rxf.at[slot], own_sem.at[0]).start()

    for b in range(chunks):
        arrive(ndev, me, lambda p: copy_o(b, p, p))

    def filt_in(i, _):
        @pl.when(c * own + i != me)
        def _():
            copy_f(s, i, c).wait_recv()

        return 0

    lax.fori_loop(0, own, filt_in, 0)
    sent(seq_count, s, lambda p: copy_h(p, s))
    for b in range(chunks):
        sent(ndev, me, lambda p: copy_a(b, p, me))
        sent(ndev, me, lambda p: copy_o(b, p, me))
    sent(seq_count, s, lambda p: copy_f(p, slot, target_c))

    @pl.when(target_c != c)
    def _():
        copy_f(s, slot, target_c).wait_send()

    @pl.when(target_c == c)
    def _():
        pltpu.make_async_copy(txf.at[s], rxf.at[slot], own_sem.at[0]).wait()

    for keep in own_o:
        keep.wait()


def finish(*refs):
    stored, drained = refs[:9], refs[9:14]
    held, made = refs[14:23], refs[23:28]
    load_sem, store_sem = refs[28:]
    loads = [
        pltpu.make_async_copy(src, dst, load_sem.at[i])
        for i, (src, dst) in enumerate(zip(stored, held))
    ]
    for load in loads:
        load.start()
    stores = [
        pltpu.make_async_copy(src, dst, store_sem.at[i])
        for i, (src, dst) in enumerate(zip(made, drained))
    ]
    rxo, perm, q_ref, k_ref, v_ref, u_ref, gain_ref, rxf, sel = held
    mix_ref, gq_ref, gk_ref, gv_ref, gf_ref = made
    local_rows, filters = q_ref.shape
    nb = local_rows // LANES
    width = perm.shape[1] // (2 * filters)
    f32 = jnp.float32
    for load in loads:
        load.wait()
    hi, lo = split(rxf[...].reshape(-1, LANES))
    for j in range(nb):
        gf_ref[:, j * LANES : (j + 1) * LANES] = mm(sel[j], hi) + mm(sel[j], lo)
    stores[4].start()
    for j in range(nb):
        r = pl.ds(j * LANES, LANES)
        if j % width == 0:
            at = j // width * 8
            hi, lo = split(rxo[:, :, at : at + 8, :].reshape(-1, LANES).T)
            both = mm(hi, perm[...]) + mm(lo, perm[...])
        at = j % width * 2 * filters
        got = both[:, at : at + 2 * filters]
        query, key = q_ref[r, :].astype(f32), k_ref[r, :].astype(f32)
        value, up = v_ref[r, :].astype(f32), u_ref[r, :].astype(f32)
        gain = gain_ref[...]
        pre = got[:, :filters] + gain * (key * value)
        back = got[:, filters:] + gain * (up * query)
        mix_ref[r, :] = (query * pre).astype(jnp.bfloat16)
        gq_ref[r, :] = (up * pre).astype(jnp.bfloat16)
        gk_ref[r, :] = (back * value).astype(jnp.bfloat16)
        gv_ref[r, :] = (back * key).astype(jnp.bfloat16)
    for store in stores[:4]:
        store.start()
    for store in stores:
        store.wait()


def local(query_proj, key_proj, value_proj, filter_taps, skip_gain, grad_mixer):
    seq_count, ch_count = lax.axis_size("seq"), lax.axis_size("ch")
    ndev = seq_count * ch_count
    local_rows, filters = filter_taps.shape
    nb = local_rows // LANES
    nf = filters // ndev
    dup = max(1, 8 // (nb * nf))
    own = filters // ch_count // nf
    tabs, sel = tables(seq_count, ch_count, nb, filters)
    chunks, part = chunking(nf)
    ab, hb = nb * 2 * part, nb * dup * nf
    f32, bf16 = jnp.float32, jnp.bfloat16
    hbm = pl.BlockSpec(memory_space=pltpu.HBM)
    dma = pltpu.SemaphoreType.DMA
    operands = (query_proj, key_proj, value_proj, grad_mixer, filter_taps, *tabs)
    home, filt = pl.pallas_call(
        functools.partial(kernel, seq_count, ch_count, nf),
        out_shape=(
            jax.ShapeDtypeStruct((chunks, ndev, ab, LANES), f32),
            jax.ShapeDtypeStruct((own, hb, LANES), f32),
        ),
        in_specs=[hbm] * len(operands),
        out_specs=(hbm,) * 2,
        scratch_shapes=[pltpu.VMEM(x.shape, x.dtype) for x in operands]
        + [
            pltpu.VMEM((chunks, ndev, ab, LANES), f32),
            pltpu.VMEM((chunks, ch_count, seq_count, ab, LANES), f32),
            pltpu.VMEM((ndev, hb, LANES), f32),
            pltpu.VMEM((seq_count, hb, LANES), f32),
            pltpu.VMEM((chunks, ch_count, seq_count, ab, LANES), f32),
            pltpu.VMEM((seq_count, hb, LANES), f32),
            dma((chunks, ndev)), dma((chunks, ndev)), dma((seq_count,)), dma((seq_count,)),
            dma((chunks, ndev)), dma((chunks, ndev)), dma((seq_count,)), dma((own,)),
            dma((len(operands),)), dma((chunks + 1,)),
        ],
        compiler_params=pltpu.CompilerParams(
            collective_id=0, has_side_effects=True, vmem_limit_bytes=VMEM_BYTES
        ),
    )(*operands)
    wide = jax.ShapeDtypeStruct((local_rows, filters), bf16)
    results = (wide, wide, wide, wide, jax.ShapeDtypeStruct((own * nf, local_rows), f32))
    operands = (
        home, tabs[0], query_proj, key_proj, value_proj, grad_mixer,
        skip_gain.reshape(1, filters), filt, sel,
    )
    *outs, grad_filter = pl.pallas_call(
        finish,
        out_shape=results,
        in_specs=[hbm] * len(operands),
        out_specs=(hbm,) * 5,
        scratch_shapes=[pltpu.VMEM(x.shape, x.dtype) for x in operands + results]
        + [dma((len(operands),)), dma((5,))],
        compiler_params=pltpu.CompilerParams(vmem_limit_bytes=VMEM_BYTES),
    )(*operands)
    return (*outs, grad_filter.T)


def solution(mesh):
    in_specs = (
        P("seq", "ch"),
        P("seq", "ch"),
        P("seq", "ch"),
        P("seq", None),
        P("ch"),
        P("seq", "ch"),
    )
    out_specs = (P("seq", "ch"), P("seq", "ch"), P("seq", "ch"), P("seq", "ch"), P("seq", "ch"))
    return jax.shard_map(local, mesh=mesh, in_specs=in_specs, out_specs=out_specs, check_vma=False)
```

```python
import functools
import math

import jax
import jax.numpy as jnp
import ml_dtypes
import numpy as np
from jax import lax
from jax.experimental import pallas as pl
from jax.experimental.pallas import tpu as pltpu
from jax.sharding import PartitionSpec as P

MESH = pl.DeviceIdType.MESH
LANES = 128
VMEM_BYTES = 64 * 2**20


def chunking(nf):
    chunks = 2 if nf % 4 == 0 else 1
    return chunks, nf // chunks


def halves(table):
    head = table.astype(np.float32).astype(ml_dtypes.bfloat16)
    tail = (table - head.astype(np.float64)).astype(np.float32).astype(ml_dtypes.bfloat16)
    return np.stack([head, tail])


@functools.lru_cache(maxsize=4)
def tables(seq_count, ch_count, nb, filters):
    ndev = seq_count * ch_count
    nf = filters // ndev
    dup = max(1, 8 // (nb * nf))
    n1 = seq_count * nb
    total = n1 * LANES
    a = np.arange(n1)
    ang = 2 * np.pi / n1 * ((a[:, None] + 0.25) * a[None, :])
    stack = np.concatenate([np.cos(ang), -np.sin(ang)], 0)
    chunks, part = chunking(nf)
    first = np.kron(stack, np.eye(2 * part))
    last = first.T / total
    stack = stack.reshape(2, n1, n1)
    owner = np.eye(nf).reshape(chunks, part, nf)
    one = np.eye(dup)[0]
    first_taps = np.einsum("rkn,bpf,q,d->rbkqpndf", stack, owner, np.ones(2), one)
    first_taps = first_taps.reshape(2 * chunks * n1 * 2 * part, n1 * dup * nf)
    last_filt = np.einsum("rkn,bpf,q,d->ndfrbkqp", stack, owner, np.eye(2)[0], np.ones(dup))
    last_filt = last_filt.reshape(n1 * dup * nf, -1) / total / math.sqrt(total)
    b = np.arange(LANES)
    turn = 2 * np.pi / total * ((a[:, None] + 0.25) * b[None, :])
    twist = np.repeat(np.stack([np.cos(turn), -np.sin(turn)]), 2 * part, axis=1)
    ang2 = 2 * np.pi / LANES * (b[:, None] * b[None, :] % LANES)
    fr, fi = np.cos(ang2), -np.sin(ang2)
    second = np.block([[fr, fi], [-fi, fr]])
    place = np.eye(filters).reshape(ndev, chunks, part, filters)
    group = max(1, 8 // (2 * part))
    perm = np.einsum("dbpc,ij,kl->bdikpjlc", place, np.eye(group), np.eye(2))
    perm = perm.reshape(chunks * ndev * group * 2 * part, group * 2 * filters)
    group = max(1, 8 // (nf * dup))
    place = np.eye(filters).reshape(ndev, nf, filters)
    perm_taps = np.einsum("dfc,ij,e->diefjc", place, np.eye(group), np.ones(dup))
    perm_taps = perm_taps.reshape(ndev * group * dup * nf, group * filters)
    own = filters // ch_count // nf
    sel = np.zeros((nb, own * nf, own, nb, dup, nf))
    for j in range(nb):
        for g in range(nf):
            for dev in range(own):
                sel[j, dev * nf + g, dev, j, 0, g] = 1.0
    bf = ml_dtypes.bfloat16
    return (
        perm.astype(bf),
        perm_taps.astype(bf),
        halves(first),
        halves(first_taps),
        halves(last),
        halves(last_filt),
        halves(second),
        halves(second.T),
        twist.astype(np.float32),
    ), sel.reshape(nb, own * nf, own * nb * dup * nf).astype(bf)


def split(x):
    head = x.astype(jnp.bfloat16)
    return head, (x - head.astype(jnp.float32)).astype(jnp.bfloat16)


def mm(x, y):
    return jnp.dot(x, y, preferred_element_type=jnp.float32)


def mm_nt(x, y):
    return lax.dot_general(x, y, (((1,), (1,)), ((), ())), preferred_element_type=jnp.float32)


def left_table(table, x):
    hi, lo = split(x)
    return mm(table[0], hi) + mm(table[0], lo) + mm(table[1], hi)


def right_table(x, table):
    hi, lo = split(x)
    return mm(hi, table[0]) + mm(lo, table[0]) + mm(hi, table[1])


def kernel(
    seq_count, ch_count, nf,
    *refs,
):
    count = (len(refs) - 18) // 2
    stored, held = refs[:count], refs[count + 2 : 2 * count + 2]
    rxo, rxf = refs[count : count + 2]
    (
        tx, rx, txh, rxh, txo, txf,
        send_a, recv_a, send_h, recv_h, send_o, recv_o, send_f, recv_f, load_sem, own_sem,
    ) = refs[2 * count + 2 :]
    q_ref, k_ref, v_ref, u_ref, h_ref, perm, perm_taps = held[:7]
    first, first_taps, last, last_filt, second, second_t, twist = held[7:]
    loads = [
        pltpu.make_async_copy(src, dst, load_sem.at[i])
        for i, (src, dst) in enumerate(zip(stored, held))
    ]
    for load in loads:
        load.start()
    ndev = seq_count * ch_count
    local_rows, filters = h_ref.shape
    nb = local_rows // LANES
    chunks, part = chunking(nf)
    q = 2 * part
    own = rxf.shape[0]
    rows = seq_count * nb * q
    s, c = lax.axis_index("seq"), lax.axis_index("ch")
    me = s * ch_count + c
    f32 = jnp.float32

    barrier = pltpu.get_barrier_semaphore()

    def greet(i, _):
        p = lax.rem(me + i, ndev)
        pl.semaphore_signal(
            barrier, inc=1, device_id=(p // ch_count, lax.rem(p, ch_count)), device_id_type=MESH
        )
        return 0

    lax.fori_loop(1, ndev, greet, 0)

    for load in loads[:7]:
        load.wait()

    def turn(table, blocks):
        hi, lo = split(jnp.concatenate(blocks, axis=1))
        return mm_nt(table[...], hi) + mm_nt(table[...], lo)

    width = perm_taps.shape[1] // filters
    for j in range(0, nb, width):
        out = turn(perm_taps, [h_ref[pl.ds((j + e) * LANES, LANES), :] for e in range(width)])
        at = j // width * 8
        txh[:, at : at + 8, :] = out.reshape(ndev, 8, LANES)

    def send_products():
        width = perm.shape[1] // (2 * filters)
        for j in range(0, nb, width):
            blocks = []
            for e in range(width):
                r = pl.ds((j + e) * LANES, LANES)
                blocks.append(k_ref[r, :].astype(f32) * v_ref[r, :].astype(f32))
                blocks.append(u_ref[r, :].astype(f32) * q_ref[r, :].astype(f32))
            at = j // width * 8
            tx[:, :, at : at + 8, :] = turn(perm, blocks).reshape(chunks, ndev, 8, LANES)

    send_products()

    def copy_a(b, p, src):
        return pltpu.make_async_remote_copy(
            src_ref=tx.at[b, p],
            dst_ref=rx.at[b, lax.rem(src, ch_count), src // ch_count],
            send_sem=send_a.at[b, p],
            recv_sem=recv_a.at[b, src],
            device_id=(p // ch_count, lax.rem(p, ch_count)),
            device_id_type=MESH,
        )

    def copy_h(p, src):
        return pltpu.make_async_remote_copy(
            src_ref=txh.at[p * ch_count + c],
            dst_ref=rxh.at[src],
            send_sem=send_h.at[p],
            recv_sem=recv_h.at[src],
            device_id=(p, c),
            device_id_type=MESH,
        )

    def copy_o(b, p, src):
        return pltpu.make_async_remote_copy(
            src_ref=txo.at[b, lax.rem(p, ch_count), p // ch_count],
            dst_ref=rxo.at[b, src],
            send_sem=send_o.at[b, p],
            recv_sem=recv_o.at[b, src],
            device_id=(p // ch_count, lax.rem(p, ch_count)),
            device_id_type=MESH,
        )

    def copy_f(p, slot, target_c):
        return pltpu.make_async_remote_copy(
            src_ref=txf.at[p],
            dst_ref=rxf.at[slot],
            send_sem=send_f.at[p],
            recv_sem=recv_f.at[slot],
            device_id=(p, target_c),
            device_id_type=MESH,
        )

    pl.semaphore_wait(barrier, ndev - 1)

    def go(count, at, make):
        def step(i, _):
            if count % 2 == 0:
                i = count // 2 + (2 * lax.rem(i, 2) - 1) * (i // 2)
            make(lax.rem(at + i, count)).start()
            return 0

        lax.fori_loop(1, count, step, 0)

    def arrive(count, at, make):
        def step(i, _):
            make(lax.rem(at + count - i, count)).wait_recv()
            return 0

        lax.fori_loop(1, count, step, 0)

    def sent(count, at, make):
        def step(i, _):
            make(lax.rem(at + i, count)).wait_send()
            return 0

        lax.fori_loop(1, count, step, 0)

    go(seq_count, s, lambda p: copy_h(p, s))
    for b in range(chunks):
        go(ndev, me, lambda p: copy_a(b, p, me))
        rx[b, c, s] = tx[b, me]
    rxh[s] = txh[me]

    for load in loads[7:]:
        load.wait()
    tr, ti = twist[0], twist[1]

    def forward(ar, ai, times):
        tr2, ti2 = jnp.concatenate([tr] * times, axis=0), jnp.concatenate([ti] * times, axis=0)
        b = jnp.concatenate([ar * tr2 - ai * ti2, ar * ti2 + ai * tr2], axis=1)
        z = right_table(b, second)
        return z[:, :LANES], z[:, LANES:]

    def backward(yr, yi, times):
        tr2, ti2 = jnp.concatenate([tr] * times, axis=0), jnp.concatenate([ti] * times, axis=0)
        y = right_table(jnp.concatenate([yr, yi], axis=1), second_t)
        yr, yi = y[:, :LANES], y[:, LANES:]
        return yr * tr2 + yi * ti2, yi * tr2 - yr * ti2

    arrive(seq_count, s, lambda p: copy_h(p, p))
    a = left_table(first_taps, rxh[...].reshape(-1, LANES))
    taps_r, taps_i = forward(a[: chunks * rows], a[chunks * rows :], chunks)
    kind = lax.rem(lax.broadcasted_iota(jnp.int32, (chunks * rows, LANES), 0), q) < part
    taps_i = jnp.where(kind, taps_i, -taps_i)

    filts_r, filts_i, own_o = [], [], []
    for b in range(chunks):
        arrive(ndev, me, lambda p: copy_a(b, p, p))
        hr, hi_ = taps_r[b * rows : (b + 1) * rows], taps_i[b * rows : (b + 1) * rows]
        hr, hi_ = jnp.concatenate([hr, hr], axis=0), jnp.concatenate([hi_, hi_], axis=0)
        filt_r = jnp.zeros((rows, LANES), f32)
        filt_i = jnp.zeros((rows, LANES), f32)
        for pair in range(0, ch_count, 2):
            x = jnp.concatenate(
                [rx[b, pair].reshape(rows, LANES), rx[b, pair + 1].reshape(rows, LANES)], axis=1
            )
            a = left_table(first, x)
            zr, zi = forward(
                jnp.concatenate([a[:rows, :LANES], a[:rows, LANES:]], axis=0),
                jnp.concatenate([a[rows:, :LANES], a[rows:, LANES:]], axis=0),
                2,
            )
            gr = pltpu.roll(zr, 2 * rows - part, 0)
            gi = pltpu.roll(zi, 2 * rows - part, 0)
            cr, ci = zr * gr + zi * gi, zr * gi - zi * gr
            filt_r = filt_r + cr[:rows] + cr[rows:]
            filt_i = filt_i + ci[:rows] + ci[rows:]
            dr, di = backward(hr * zr - hi_ * zi, hr * zi + hi_ * zr, 2)
            d = jnp.concatenate(
                [
                    jnp.concatenate([dr[:rows], dr[rows:]], axis=1),
                    jnp.concatenate([di[:rows], di[rows:]], axis=1),
                ],
                axis=0,
            )
            out = left_table(last, d)
            txo[b, pair] = out[:, :LANES].reshape(txo.shape[2:])
            txo[b, pair + 1] = out[:, LANES:].reshape(txo.shape[2:])
        filts_r.append(filt_r)
        filts_i.append(filt_i)
        go(ndev, me, lambda p: copy_o(b, p, me))
        keep = pltpu.make_async_copy(txo.at[b, c, s], rxo.at[b, me], own_sem.at[b + 1])
        keep.start()
        own_o.append(keep)

    dr, di = backward(
        jnp.concatenate(filts_r, axis=0), jnp.concatenate(filts_i, axis=0), chunks
    )
    out = left_table(last_filt, jnp.concatenate([dr, di], axis=0))
    txf[...] = out.reshape(txf.shape)
    slot, target_c = lax.rem(me, own), me // own

    go(seq_count, s, lambda p: copy_f(p, slot, target_c))

    @pl.when(target_c != c)
    def _():
        copy_f(s, slot, target_c).start()

    @pl.when(target_c == c)
    def _():
        pltpu.make_async_copy(txf.at[s], rxf.at[slot], own_sem.at[0]).start()

    for b in range(chunks):
        arrive(ndev, me, lambda p: copy_o(b, p, p))

    def filt_in(i, _):
        @pl.when(c * own + i != me)
        def _():
            copy_f(s, i, c).wait_recv()

        return 0

    lax.fori_loop(0, own, filt_in, 0)
    sent(seq_count, s, lambda p: copy_h(p, s))
    for b in range(chunks):
        sent(ndev, me, lambda p: copy_a(b, p, me))
        sent(ndev, me, lambda p: copy_o(b, p, me))
    sent(seq_count, s, lambda p: copy_f(p, slot, target_c))

    @pl.when(target_c != c)
    def _():
        copy_f(s, slot, target_c).wait_send()

    @pl.when(target_c == c)
    def _():
        pltpu.make_async_copy(txf.at[s], rxf.at[slot], own_sem.at[0]).wait()

    for keep in own_o:
        keep.wait()


def finish(*refs):
    stored, drained = refs[:9], refs[9:14]
    held, made = refs[14:23], refs[23:28]
    load_sem, store_sem = refs[28:]
    loads = [
        pltpu.make_async_copy(src, dst, load_sem.at[i])
        for i, (src, dst) in enumerate(zip(stored, held))
    ]
    for load in loads:
        load.start()
    stores = [
        pltpu.make_async_copy(src, dst, store_sem.at[i])
        for i, (src, dst) in enumerate(zip(made, drained))
    ]
    rxo, perm, q_ref, k_ref, v_ref, u_ref, gain_ref, rxf, sel = held
    mix_ref, gq_ref, gk_ref, gv_ref, gf_ref = made
    local_rows, filters = q_ref.shape
    nb = local_rows // LANES
    width = perm.shape[1] // (2 * filters)
    f32 = jnp.float32
    for load in loads:
        load.wait()
    hi, lo = split(rxf[...].reshape(-1, LANES))
    for j in range(nb):
        gf_ref[:, j * LANES : (j + 1) * LANES] = mm(sel[j], hi) + mm(sel[j], lo)
    stores[4].start()
    for j in range(nb):
        r = pl.ds(j * LANES, LANES)
        if j % width == 0:
            at = j // width * 8
            hi, lo = split(rxo[:, :, at : at + 8, :].reshape(-1, LANES).T)
            both = mm(hi, perm[...]) + mm(lo, perm[...])
        at = j % width * 2 * filters
        got = both[:, at : at + 2 * filters]
        query, key = q_ref[r, :].astype(f32), k_ref[r, :].astype(f32)
        value, up = v_ref[r, :].astype(f32), u_ref[r, :].astype(f32)
        gain = gain_ref[...]
        pre = got[:, :filters] + gain * (key * value)
        back = got[:, filters:] + gain * (up * query)
        mix_ref[r, :] = (query * pre).astype(jnp.bfloat16)
        gq_ref[r, :] = (up * pre).astype(jnp.bfloat16)
        gk_ref[r, :] = (back * value).astype(jnp.bfloat16)
        gv_ref[r, :] = (back * key).astype(jnp.bfloat16)
    for store in stores[:4]:
        store.start()
    for store in stores:
        store.wait()


def local(query_proj, key_proj, value_proj, filter_taps, skip_gain, grad_mixer):
    seq_count, ch_count = lax.axis_size("seq"), lax.axis_size("ch")
    ndev = seq_count * ch_count
    local_rows, filters = filter_taps.shape
    nb = local_rows // LANES
    nf = filters // ndev
    dup = max(1, 8 // (nb * nf))
    own = filters // ch_count // nf
    tabs, sel = tables(seq_count, ch_count, nb, filters)
    chunks, part = chunking(nf)
    ab, hb = nb * 2 * part, nb * dup * nf
    f32, bf16 = jnp.float32, jnp.bfloat16
    hbm = pl.BlockSpec(memory_space=pltpu.HBM)
    dma = pltpu.SemaphoreType.DMA
    operands = (query_proj, key_proj, value_proj, grad_mixer, filter_taps, *tabs)
    home, filt = pl.pallas_call(
        functools.partial(kernel, seq_count, ch_count, nf),
        out_shape=(
            jax.ShapeDtypeStruct((chunks, ndev, ab, LANES), f32),
            jax.ShapeDtypeStruct((own, hb, LANES), f32),
        ),
        in_specs=[hbm] * len(operands),
        out_specs=(hbm,) * 2,
        scratch_shapes=[pltpu.VMEM(x.shape, x.dtype) for x in operands]
        + [
            pltpu.VMEM((chunks, ndev, ab, LANES), f32),
            pltpu.VMEM((chunks, ch_count, seq_count, ab, LANES), f32),
            pltpu.VMEM((ndev, hb, LANES), f32),
            pltpu.VMEM((seq_count, hb, LANES), f32),
            pltpu.VMEM((chunks, ch_count, seq_count, ab, LANES), f32),
            pltpu.VMEM((seq_count, hb, LANES), f32),
            dma((chunks, ndev)), dma((chunks, ndev)), dma((seq_count,)), dma((seq_count,)),
            dma((chunks, ndev)), dma((chunks, ndev)), dma((seq_count,)), dma((own,)),
            dma((len(operands),)), dma((chunks + 1,)),
        ],
        compiler_params=pltpu.CompilerParams(
            collective_id=0, has_side_effects=True, vmem_limit_bytes=VMEM_BYTES
        ),
    )(*operands)
    wide = jax.ShapeDtypeStruct((local_rows, filters), bf16)
    results = (wide, wide, wide, wide, jax.ShapeDtypeStruct((own * nf, local_rows), f32))
    operands = (
        home, tabs[0], query_proj, key_proj, value_proj, grad_mixer,
        skip_gain.reshape(1, filters), filt, sel,
    )
    *outs, grad_filter = pl.pallas_call(
        finish,
        out_shape=results,
        in_specs=[hbm] * len(operands),
        out_specs=(hbm,) * 5,
        scratch_shapes=[pltpu.VMEM(x.shape, x.dtype) for x in operands + results]
        + [dma((len(operands),)), dma((5,))],
        compiler_params=pltpu.CompilerParams(vmem_limit_bytes=VMEM_BYTES),
    )(*operands)
    return (*outs, grad_filter.T)


def solution(mesh):
    in_specs = (
        P("seq", "ch"),
        P("seq", "ch"),
        P("seq", "ch"),
        P("seq", None),
        P("ch"),
        P("seq", "ch"),
    )
    out_specs = (P("seq", "ch"), P("seq", "ch"), P("seq", "ch"), P("seq", "ch"), P("seq", "ch"))
    return jax.shard_map(local, mesh=mesh, in_specs=in_specs, out_specs=out_specs, check_vma=False)
```
